32 devices in a mesh: dp: 2 (over x), ctx: 8 (over z, core), head: 2 (over y).
Axes of the slice: x: 2, y: 2, z: 4, core: 2. Of those that a mesh axis runs over, the one named last changes fastest.
Arguments:
- queries: bfloat16 [1024, 4, 1024], P('ctx', ('dp', 'head')), may hold values from -5 to 5
- keys: bfloat16 [1024, 4, 128], P(('ctx', 'head', 'dp')), may hold values from -5 to 5
- values: bfloat16 [1024, 4, 128], P(('ctx', 'head', 'dp')), may hold values from -6 to 6
- outputs: bfloat16 [1024, 4, 1024], P('ctx', ('dp', 'head')), may hold values from -3 to 3
- grad_out: bfloat16 [1024, 4, 1024], P('ctx', ('dp', 'head')), may hold values from -6 to 6
- doc_ids: int32 [1024], P('ctx'), may hold values from 0 to 3, never falling along the last dimension, each value on 1 to 512 neighbouring positions
- owner: int32 [32], P('ctx'), may hold values from 0 to 7, as said below
Outputs:
- grad_q_planned: bfloat16 [1024, 4, 1024], P('ctx', ('dp', 'head'))
- grad_k: bfloat16 [1024, 4, 128], P('ctx', ('dp', 'head'))
- grad_v: bfloat16 [1024, 4, 128], P('ctx', ('dp', 'head'))
The draws below stay inside these ranges and needn't reach their ends.
Inputs may be any that keep to these rules, and one draw needn't show every extreme that they name: `owner`: blocks b with the same b // 4 have different owners, and blocks with the same b % 4 have different owners, so every index of ctx owns exactly 4 blocks, one for each value of b % 4.
All inputs are finite; a program needn't handle non-finite values.
Results may differ from the reference program's by a relative error of at most 0.0047.
The reference program's roundings to bfloat16 on the way (of `probs_low`, `dscore` and `grad_q`) count: a program that leaves them out, or rounds other values in their place, can miss the bound.
Values may be sent and summed in bfloat16 or wider, within the bound.
A program may use at most 64 MiB of HBM per device.

```python
import math
import jax
import jax.numpy as jnp
import numpy as np
from jax import lax

HD = 128
KVH = 4
GROUP = 8
TOK_DEV = 128
CPD = 4
L = 1024
BLK = 32
NBLK = 32
DOCS = 4


def draw_keys(key, part):
    base = jax.random.normal(jax.random.fold_in(key, 31), (L, KVH, HD), jnp.float32)
    base = jnp.clip(base, -4.0, 4.0)
    return base.astype(jnp.bfloat16)


def draw_queries(key, part):
    base = jax.random.normal(jax.random.fold_in(key, 41), (L, KVH, GROUP * HD), jnp.float32)
    base = jnp.clip(base, -4.0, 4.0)
    return base.astype(jnp.bfloat16)


def draw_owner(key, part):
    peer_count = L // TOK_DEV
    per_device = TOK_DEV // BLK
    first = jax.random.permutation(jax.random.fold_in(key, 11), peer_count)
    second = jax.random.permutation(jax.random.fold_in(key, 12), peer_count)
    offsets = jax.random.permutation(jax.random.fold_in(key, 13), peer_count)[:per_device]
    block_ids = jnp.arange(NBLK, dtype=jnp.int32)
    anchor = block_ids // per_device
    local_slot = block_ids % per_device
    return first[(second[anchor] + offsets[local_slot]) % peer_count].astype(jnp.int32)


def shard_levels(stream_key, shape, cuts, low, high):
    level, own = 1.0, jax.random.fold_in(stream_key, 6)
    for axis_at, shards_of in cuts:
        heights = jnp.exp(jax.random.uniform(jax.random.fold_in(own, axis_at), (shards_of,), jnp.float32, low / len(cuts), high / len(cuts)))
        level = level * jnp.repeat(heights, shape[axis_at] // shards_of).reshape([-1 if axis == axis_at else 1 for axis in range(len(shape))])
    return level


def split_up(amount, total, reach, skew):
    loads = [(1 << 20) // math.isqrt(rank ** skew) + 1 for rank in range(2, amount + 1)]
    spare, counts = total - reach - (amount - 1), [1] * (amount - 1)
    while spare > 0:
        free = [i for i in range(amount - 1) if counts[i] < reach]
        mass, remaining = sum([loads[i] for i in free]), spare
        for i in free:
            addition = min(reach - counts[i], max(1, remaining * loads[i] // mass), spare)
            counts[i] = counts[i] + addition
            spare = spare - addition
    return np.array([reach] + counts)


def ragged_sizes(rng, number_of, total, reach, slope):
    if number_of == 2:
        one = jax.random.randint(rng, (), max(1, total - reach), min(reach, total - 1) + 1)
        return jnp.stack([one, total - one])
    sizes = jnp.asarray(split_up(number_of, total, reach, slope), jnp.int32)
    pairs = (number_of - 1) // 2
    donor, sink = sizes[1:1 + 2 * pairs:2], sizes[2:2 + 2 * pairs:2]
    margin = jnp.minimum(donor - 1, reach - sink)
    moved = jax.random.randint(jax.random.fold_in(rng, 1), (pairs,), 0, 1 << 20) % (margin + 1)
    sizes = sizes.at[1:1 + 2 * pairs:2].set(donor - moved).at[2:2 + 2 * pairs:2].set(sink + moved)
    return sizes[jax.random.permutation(jax.random.fold_in(rng, 2), number_of)]


def gaussian(stream_key, dims, spread, bound, split=(), kind=jnp.bfloat16):
    factor_of = shard_levels(stream_key, dims, split, -0.22, 0.18) if split else 1.0
    values = jax.random.normal(stream_key, dims, jnp.float32) * spread * factor_of
    return jnp.minimum(jnp.maximum(values, -bound), bound).astype(kind)


def setup_inputs(seed: int = 0) -> dict:
    key_list = jax.random.split(jax.random.key(seed), 8)
    queries = draw_queries(jax.random.fold_in(key_list[7], 71), 0)
    keys = draw_keys(jax.random.fold_in(key_list[7], 71), 0)
    values = gaussian(key_list[2], (L, KVH, HD), 1.0, 6.0, ((0, 32),))
    outputs = gaussian(key_list[3], (L, KVH, GROUP * HD), 0.5, 3.0, ((0, 8), (1, 4)))
    grad_out = gaussian(key_list[4], (L, KVH, GROUP * HD), 1.0, 6.0, ((0, 8), (1, 4)))
    doc_ids = jnp.searchsorted(jnp.cumsum(ragged_sizes(key_list[5], DOCS, L, L // 2, 0)), jnp.arange(L), side="right").astype(jnp.int32)
    owner = draw_owner(jax.random.fold_in(key_list[7], 71), 0)
    return {"queries": queries, "keys": keys, "values": values, "outputs": outputs, "grad_out": grad_out, "doc_ids": doc_ids, "owner": owner}


def reference(queries, keys, values, outputs, grad_out, doc_ids, owner):
    scale_val = HD ** -0.5
    q_block = min(256, L)
    block_total = L // q_block
    positions = jnp.arange(L, dtype=jnp.int32)
    high = lax.Precision.HIGHEST
    q_heads = jnp.transpose(queries, (1, 0, 2)).reshape(KVH, L, GROUP, HD)
    o_heads = jnp.transpose(outputs, (1, 0, 2)).reshape(KVH, L, GROUP, HD)
    do_heads = jnp.transpose(grad_out, (1, 0, 2)).reshape(KVH, L, GROUP, HD)
    k_heads = jnp.transpose(keys, (1, 0, 2))
    v_heads = jnp.transpose(values, (1, 0, 2))

    def per_group(members):
        q_grp, k_grp, v_grp, o_grp, do_grp = members
        k_full = k_grp.astype(jnp.float32)
        v_full = v_grp.astype(jnp.float32)

        def per_block(state, block_index):
            dk_sum, dv_sum = state
            row_start = block_index * q_block
            q_rows = lax.dynamic_slice_in_dim(q_grp, row_start, q_block, 0).astype(jnp.float32)
            do_rows = lax.dynamic_slice_in_dim(do_grp, row_start, q_block, 0).astype(jnp.float32)
            o_rows = lax.dynamic_slice_in_dim(o_grp, row_start, q_block, 0).astype(jnp.float32)
            row_pos = row_start + jnp.arange(q_block, dtype=jnp.int32)
            row_doc = lax.dynamic_slice_in_dim(doc_ids, row_start, q_block, 0)
            visible = ((doc_ids[None, :] == row_doc[:, None]) & (positions[None, :] <= row_pos[:, None]))[None]
            scores = jnp.einsum("rid,kd->irk", q_rows, k_full, precision=high) * scale_val
            peak = jnp.max(jnp.where(visible, scores, -jnp.inf), axis=-1, keepdims=True)
            total = jnp.sum(jnp.where(visible, jnp.exp(scores - peak), 0.0), axis=-1, keepdims=True)
            lse = peak + jnp.log(total)
            probs = jnp.where(visible, jnp.exp(scores - lse), 0.0)
            probs_low = probs.astype(jnp.bfloat16)
            dprob = jnp.einsum("rid,kd->irk", do_rows, v_full, precision=high)
            delta = jnp.transpose(jnp.sum(do_rows * o_rows, axis=-1), (1, 0))[..., None]
            dscore = (probs * (dprob - delta) * scale_val).astype(jnp.bfloat16)
            ds_wide = dscore.astype(jnp.float32)
            dq_rows = jnp.einsum("irk,kd->rid", ds_wide, k_full, precision=high)
            dk_sum = dk_sum + jnp.einsum("irk,rid->kd", ds_wide, q_rows, precision=high)
            dv_sum = dv_sum + jnp.einsum("irk,rid->kd", probs_low.astype(jnp.float32), do_rows, precision=high)
            return (dk_sum, dv_sum), dq_rows.astype(jnp.bfloat16)

        zeros_kd = jnp.zeros((L, HD), jnp.float32)
        (dk_grp, dv_grp), dq_blocks = lax.scan(per_block, (zeros_kd, zeros_kd), jnp.arange(block_total, dtype=jnp.int32))
        return dq_blocks.reshape(L, GROUP * HD), dk_grp, dv_grp

    dq_all, dk_all, dv_all = lax.map(per_group, (q_heads, k_heads, v_heads, o_heads, do_heads))
    grad_q = jnp.transpose(dq_all, (1, 0, 2))
    blocks = grad_q.reshape(NBLK, BLK, KVH, GROUP * HD)
    target = owner * CPD + jnp.arange(NBLK, dtype=jnp.int32) % CPD
    planned = jnp.zeros_like(blocks).at[target].set(blocks).reshape(L, KVH, GROUP * HD)
    grad_k = jnp.transpose(dk_all, (1, 0, 2)).astype(jnp.bfloat16)
    grad_v = jnp.transpose(dv_all, (1, 0, 2)).astype(jnp.bfloat16)
    return planned, grad_k, grad_v
```

```python
import functools

import jax
import jax.numpy as jnp
from jax import lax
from jax.experimental import pallas as pl
from jax.experimental.pallas import tpu as pltpu
from jax.sharding import PartitionSpec as P

NEG_FILL = -1e30
MESH = pl.DeviceIdType.MESH


def each(low, high, step):
    if high - low <= 8:
        for i in range(low, high):
            step(i)
    else:
        lax.fori_loop(low, high, lambda i, carry: (step(i), carry)[1], 0)


def dot(a, b, ca, cb):
    return lax.dot_general(
        a, b, (((ca,), (cb,)), ((), ())), preferred_element_type=jnp.float32
    )


def kernel(
    cfg, q_hbm, do_hbm, o_hbm, kv_ref, info_ref, dq_out, dk_out, dv_out,
    q_buf, do_buf, o_buf, kv_buf, info_buf, bias, send_mat, pick_mat, delta,
    scores, acc, dq_send, dq_recv, dkv_send, dkv_recv,
    load_sem, kv_ssem, kv_rsem, info_ssem, info_rsem, dq_ssem, dq_rsem,
    dkv_ssem, dkv_rsem,
):
    dp_n, ctx_n, head_n, back, chunk, block_len = cfg
    rows, width = q_buf.shape
    hd = kv_ref.shape[-1]
    piece = kv_ref.shape[2]
    pairs = dq_send.shape[0]
    blk_pad = dq_send.shape[2]
    wide = dq_send.shape[3]
    per_pair = wide // hd
    scale_val = hd ** (-0.5)
    chunks = (back + 1) * rows // chunk
    dp, ctx, head = lax.axis_index("dp"), lax.axis_index("ctx"), lax.axis_index("head")
    cols = dp_n * head_n
    my_col = dp * head_n + head
    my_piece = head * dp_n + dp

    loads = [
        pltpu.make_async_copy(src, dst, load_sem.at[i])
        for i, (src, dst) in enumerate(((q_hbm, q_buf), (do_hbm, do_buf), (o_hbm, o_buf)))
    ]
    for load in loads:
        load.start()

    barrier = pltpu.get_barrier_semaphore()
    everyone = dp_n * ctx_n * head_n
    me = (dp * ctx_n + ctx) * head_n + head

    def greet(k):
        t = lax.rem(me + k, everyone)
        pl.semaphore_signal(
            barrier, inc=1,
            device_id={"dp": t // (ctx_n * head_n), "ctx": lax.rem(t // head_n, ctx_n), "head": lax.rem(t, head_n)},
            device_id_type=MESH,
        )

    lax.fori_loop(1, everyone, lambda k, c: (greet(k), c)[1], 0)

    kv_buf[:, pl.ds(pl.multiple_of(my_piece * piece, piece), piece), :] = kv_ref[my_col]
    info_buf[ctx] = info_ref[...]
    for_missing = lambda s: pl.when(ctx < s)(
        lambda: kv_buf.__setitem__(
            (slice(None), pl.ds(pl.multiple_of(s * rows, rows), rows), slice(None)),
            jnp.zeros((2, rows, hd), kv_buf.dtype),
        )
    )
    each(1, back + 1, for_missing)
    pl.semaphore_wait(barrier, everyone - 1)

    def info_copy(d):
        return pltpu.make_async_remote_copy(
            src_ref=info_ref, dst_ref=info_buf.at[ctx],
            send_sem=info_ssem.at[d], recv_sem=info_rsem.at[d],
            device_id={"ctx": lax.rem(ctx + d, ctx_n)}, device_id_type=MESH,
        )

    def kv_copy(s, k, target_ctx):
        t = lax.rem(my_col + k, cols)
        return pltpu.make_async_remote_copy(
            src_ref=kv_ref.at[t],
            dst_ref=kv_buf.at[:, pl.ds(pl.multiple_of(s * rows + my_piece * piece, piece), piece), :],
            send_sem=kv_ssem.at[s, k], recv_sem=kv_rsem.at[s, k],
            device_id={"dp": t // head_n, "ctx": target_ctx, "head": lax.rem(t, head_n)}, device_id_type=MESH,
        )

    def kv_start(s):
        def go():
            for k in range(cols):
                if isinstance(s, int) and s == 0 and k == 0:
                    continue
                kv_copy(s, k, lax.rem(ctx + s, ctx_n)).start()
        pl.when(ctx + s < ctx_n)(go)

    def kv_wait(s):
        def go():
            for k in range(cols):
                if isinstance(s, int) and s == 0 and k == 0:
                    continue
                frm = lax.rem(my_col + cols - k, cols)
                place = lax.rem(frm, head_n) * dp_n + frm // head_n
                pltpu.make_async_copy(
                    kv_ref.at[0],
                    kv_buf.at[:, pl.ds(pl.multiple_of(s * rows + place * piece, piece), piece), :],
                    kv_rsem.at[s, k],
                ).wait()
        pl.when(ctx >= s)(go)

    def kv_sent(s):
        def go():
            for k in range(cols):
                if isinstance(s, int) and s == 0 and k == 0:
                    continue
                kv_copy(s, k, lax.rem(ctx + s, ctx_n)).wait_send()
        pl.when(ctx + s < ctx_n)(go)

    each(1, ctx_n, lambda d: info_copy(d).start())
    kv_start(0)
    each(1, back + 1, kv_start)

    for load in loads:
        load.wait()

    def stacked(buf, p):
        return jnp.concatenate(
            [buf[:, (p * per_pair + i) * hd:(p * per_pair + i + 1) * hd] for i in range(per_pair)], axis=0
        )

    for p in range(pairs):
        prod = stacked(do_buf, p).astype(jnp.float32) * stacked(o_buf, p).astype(jnp.float32)
        delta[p] = jnp.sum(prod.T, axis=0, keepdims=True)

    tok = lax.broadcasted_iota(jnp.int32, (blk_pad, rows), 1)
    sub = lax.broadcasted_iota(jnp.int32, (blk_pad, rows), 0)
    same_row = lax.rem(tok, block_len) == sub

    def fill_send(p):
        hit = jnp.broadcast_to(info_ref[1:2, :], (blk_pad, rows)) == p
        at = pl.multiple_of(p * blk_pad, blk_pad)
        send_mat[pl.ds(at, blk_pad), :] = jnp.where(hit & same_row, 1.0, 0.0).astype(send_mat.dtype)

    each(0, ctx_n, fill_send)
    each(1, ctx_n, lambda d: info_copy(d).wait_recv())

    def fill_pick(p):
        hit = jnp.broadcast_to(info_buf[p, 1:2, :], (blk_pad, rows)) == ctx
        at = pl.multiple_of(p * blk_pad, blk_pad)
        pick_mat[pl.ds(at, blk_pad), :] = jnp.where(hit & same_row, 1.0, 0.0).astype(pick_mat.dtype)

    each(0, ctx_n, fill_pick)
    my_doc = jnp.broadcast_to(info_ref[0:1, :], (rows, rows)).astype(jnp.float32)
    key_at = lax.broadcasted_iota(jnp.int32, (rows, rows), 0)
    query_at = lax.broadcasted_iota(jnp.int32, (rows, rows), 1)

    def fill_bias(s):
        src = lax.rem(ctx + ctx_n - s, ctx_n)
        key_doc = jnp.broadcast_to(info_buf[src, 0:1, :], (rows, rows)).astype(jnp.float32).T
        first = jnp.where(ctx >= s, key_at - s * rows, rows)
        seen = (key_doc == my_doc) & (first <= query_at)
        bias[pl.ds(pl.multiple_of(s * rows, rows), rows), :] = jnp.where(seen, 0.0, NEG_FILL)

    each(0, back + 1, fill_bias)
    kv_wait(0)
    each(1, back + 1, kv_wait)

    def dq_copy(p, d):
        t = lax.rem(ctx + d, ctx_n)
        return pltpu.make_async_remote_copy(
            src_ref=dq_send.at[p, t], dst_ref=dq_recv.at[p, ctx],
            send_sem=dq_ssem.at[p, d], recv_sem=dq_rsem.at[p, d],
            device_id={"ctx": t}, device_id_type=MESH,
        )

    def span(i):
        return pl.ds(pl.multiple_of(i * chunk, chunk), chunk)

    def loop(step, start):
        return step(0, start) if chunks == 1 else lax.fori_loop(0, chunks, step, start)

    for p in range(pairs):
        q_p, do_p = stacked(q_buf, p), stacked(do_buf, p)
        delta_p = delta[p]

        def raw(i, peak):
            s = dot(kv_buf[0, span(i), :], q_p, 1, 1) * scale_val
            s = s + jnp.concatenate([bias[span(i), :]] * per_pair, axis=1)
            scores[span(i), :] = s
            return jnp.maximum(peak, jnp.max(s, axis=0, keepdims=True))

        peak = loop(raw, jnp.full((1, wide), NEG_FILL, jnp.float32))

        def weigh(i, total):
            e = jnp.exp(scores[span(i), :] - peak)
            scores[span(i), :] = e
            return total + jnp.sum(e, axis=0, keepdims=True)

        share = 1.0 / loop(weigh, jnp.zeros((1, wide), jnp.float32))

        def grads(i, dq_sum):
            probs = scores[span(i), :] * share
            dprob = dot(kv_buf[1, span(i), :], do_p, 1, 1)
            dscore = (probs * (dprob - delta_p) * scale_val).astype(jnp.bfloat16)
            dk = dot(dscore, q_p, 1, 0)
            dv = dot(probs.astype(jnp.bfloat16), do_p, 1, 0)
            if p > 0:
                dk = dk + acc[0, span(i), :]
                dv = dv + acc[1, span(i), :]
            acc[0, span(i), :] = dk
            acc[1, span(i), :] = dv
            return dq_sum + dot(kv_buf[0, span(i), :], dscore, 0, 0)

        dq_t = loop(grads, jnp.zeros((hd, wide), jnp.float32)).astype(jnp.bfloat16)
        for i in range(per_pair):
            out = dot(send_mat[...], dq_t[:, i * rows:(i + 1) * rows], 1, 1).astype(jnp.bfloat16)
            dq_send[p, :, :, i * hd:(i + 1) * hd] = out.reshape(ctx_n, blk_pad, hd)
        each(1, ctx_n, lambda d: dq_copy(p, d).start())

    def dkv_copy(s):
        return pltpu.make_async_remote_copy(
            src_ref=dkv_send.at[s], dst_ref=dkv_recv.at[s],
            send_sem=dkv_ssem.at[s], recv_sem=dkv_rsem.at[s],
            device_id={"ctx": lax.rem(ctx + ctx_n - s, ctx_n)}, device_id_type=MESH,
        )

    def dkv_start(s):
        def go():
            at = pl.ds(pl.multiple_of(s * rows, rows), rows)
            dkv_send[s] = acc[:, at, :].astype(dkv_send.dtype)
            dkv_copy(s).start()
        pl.when(ctx >= s)(go)

    each(1, back + 1, dkv_start)

    for p in range(pairs):
        dq_recv[p, ctx] = dq_send[p, ctx]
        each(1, ctx_n, lambda d: dq_copy(p, d).wait_recv())
        parts = dq_recv[p].reshape(ctx_n * blk_pad, wide)
        dq_out[:, p * wide:(p + 1) * wide] = dot(pick_mat[...], parts, 0, 0).astype(dq_out.dtype)

    def dkv_add(s):
        def go():
            dkv_copy(s).wait_recv()
            acc[:, 0:rows, :] = acc[:, 0:rows, :] + dkv_recv[s].astype(jnp.float32)
        pl.when(ctx + s < ctx_n)(go)

    each(1, back + 1, dkv_add)
    dk_out[...] = acc[0, 0:rows, :].astype(dk_out.dtype)
    dv_out[...] = acc[1, 0:rows, :].astype(dv_out.dtype)

    kv_sent(0)
    each(1, back + 1, kv_sent)
    each(1, ctx_n, lambda d: info_copy(d).wait_send())
    for p in range(pairs):
        each(1, ctx_n, lambda d: dq_copy(p, d).wait_send())
    each(1, back + 1, lambda s: pl.when(ctx >= s)(lambda: dkv_copy(s).wait_send()))


def body(sizes, queries, keys, values, outputs, grad_out, doc_ids, owner):
    dp_n, ctx_n, head_n = sizes
    rows, _, width = queries.shape
    piece, _, hd = keys.shape
    per_device = owner.shape[0]
    block_len = rows // per_device
    blk_pad = max(block_len, 16)
    group = width // hd
    per_pair = min(2, group)
    pairs, wide = group // per_pair, per_pair * hd
    reach = rows * ctx_n // 2
    back = min(ctx_n - 1, (reach - 1 + rows - 1) // rows)
    take = max(n for n in range(1, 6) if (back + 1) % n == 0)
    keys_seen = (back + 1) * rows

    kv = jnp.transpose(jnp.stack([keys, values]), (2, 0, 1, 3))
    info = jnp.concatenate(
        [doc_ids[None], jnp.repeat(owner, block_len)[None], jnp.zeros((6, rows), jnp.int32)]
    )
    cols = dp_n * head_n
    any_space = pl.BlockSpec(memory_space=pl.ANY)
    vmem = pl.BlockSpec(memory_space=pltpu.VMEM)
    bf16, f32 = jnp.bfloat16, jnp.float32
    dma = pltpu.SemaphoreType.DMA
    outs = pl.pallas_call(
        functools.partial(kernel, (dp_n, ctx_n, head_n, back, take * rows, block_len)),
        out_shape=(
            jax.ShapeDtypeStruct((rows, width), bf16),
            jax.ShapeDtypeStruct((rows, hd), bf16),
            jax.ShapeDtypeStruct((rows, hd), bf16),
        ),
        in_specs=[any_space] * 3 + [vmem] * 2,
        out_specs=(vmem, vmem, vmem),
        scratch_shapes=[
            pltpu.VMEM((rows, width), bf16),
            pltpu.VMEM((rows, width), bf16),
            pltpu.VMEM((rows, width), bf16),
            pltpu.VMEM((2, keys_seen, hd), bf16),
            pltpu.VMEM((ctx_n,) + info.shape, jnp.int32),
            pltpu.VMEM((keys_seen, rows), f32),
            pltpu.VMEM((ctx_n * blk_pad, rows), bf16),
            pltpu.VMEM((ctx_n * blk_pad, rows), bf16),
            pltpu.VMEM((pairs, 1, wide), f32),
            pltpu.VMEM((keys_seen, wide), f32),
            pltpu.VMEM((2, keys_seen, hd), f32),
            pltpu.VMEM((pairs, ctx_n, blk_pad, wide), bf16),
            pltpu.VMEM((pairs, ctx_n, blk_pad, wide), bf16),
            pltpu.VMEM((back + 1, 2, rows, hd), bf16),
            pltpu.VMEM((back + 1, 2, rows, hd), bf16),
            dma((3,)),
            dma((back + 1, cols)), dma((back + 1, cols)),
            dma((ctx_n,)), dma((ctx_n,)),
            dma((pairs, ctx_n)), dma((pairs, ctx_n)),
            dma((back + 1,)), dma((back + 1,)),
        ],
        compiler_params=pltpu.CompilerParams(
            collective_id=0, has_side_effects=True, vmem_limit_bytes=40 * 2**20
        ),
    )(*(a.reshape(rows, width) for a in (queries, grad_out, outputs)), kv, info)
    return tuple(out[:, None, :] for out in outs)


def solution(mesh):
    placed = (
        P("ctx", ("dp", "head"), None),
        P(("ctx", "head", "dp"), None, None),
        P(("ctx", "head", "dp"), None, None),
        P("ctx", ("dp", "head"), None),
        P("ctx", ("dp", "head"), None),
        P("ctx"),
        P("ctx"),
    )
    sizes = tuple(mesh.shape[name] for name in ("dp", "ctx", "head"))
    return jax.shard_map(
        functools.partial(body, sizes),
        mesh=mesh,
        in_specs=placed,
        out_specs=(P("ctx", ("dp", "head"), None),) * 3,
        check_vma=False,
    )
```
